32 devices in a mesh: groups: 2 (over y), gx: 16 (over z, x, core).
Axes of the slice: x: 2, y: 2, z: 4, core: 2. Of those that a mesh axis runs over, the one named last changes fastest.
Arguments:
- node_feats: bfloat16 [8192, 512], P(('groups', 'gx')), parts along dimension 0, may hold values from -6 to 6
- cotangent: bfloat16 [8192, 512], P(('groups', 'gx')), parts along dimension 0, may hold values from -6 to 6
- tile_val: bfloat16 [64, 4, 128, 128], P(('groups', 'gx')), parts along dimension 0, may hold values from -0.25 to 0.25
- tile_src: int32 [64, 4], P(('groups', 'gx')), parts along dimension 0, may hold values from 0 to 3
- halo_list: int32 [32, 2, 1], P(('groups', 'gx')), parts along dimension 0, may hold values from 0 to 1, as said below
- block_count: int32 [32], P(('groups', 'gx')), parts along dimension 0, may hold values from 1 to 2, as said below
- coarse_src: int32 [64, 4], P(('groups', 'gx')), parts along dimension 0, may hold values from 0 to 3
- coarse_val: float32 [64, 4], P(('groups', 'gx')), parts along dimension 0, may hold values from -3 to 3
- w_self: bfloat16 [2, 512, 512], replicated, may hold values from -0.25 to 0.25
- w_agg: bfloat16 [2, 512, 512], replicated, may hold values from -0.25 to 0.25
- w_out: bfloat16 [2, 512, 512], replicated, may hold values from -0.25 to 0.25
- norm_gain: float32 [2, 512], replicated, may hold values from 0.5 to 1.5
Outputs:
- out_feats: bfloat16 [8192, 512], P(('groups', 'gx')), parts along dimension 0
- feats_grad: bfloat16 [8192, 512], P(('groups', 'gx')), parts along dimension 0
- self_grad: bfloat16 [4, 512, 512], P('groups'), parts along dimension 0
- agg_grad: bfloat16 [4, 512, 512], P('groups'), parts along dimension 0
- out_grad: bfloat16 [4, 512, 512], P('groups'), parts along dimension 0
- gain_grad: float32 [4, 512], P('groups'), parts along dimension 0
The draws below stay inside these ranges and needn't reach their ends.
There are 2 independent parts, one for each index of `groups`. The reference program is written for one: setup_inputs(seed, part) draws one part's arguments, and reference() takes and returns one part's arrays. A program takes and returns all parts, laid end to end along the dimension named above; an argument that names none is the same for every part. Nothing has to cross between parts.
Inputs may be any that keep to these rules, and one draw needn't show every extreme that they name: block_count is reached at both ends: some partition has 2 blocks and some has 1. halo_list[p, s, j] names a block of partition p below block_count[p]; blocks may repeat.
All inputs are finite; a program needn't handle non-finite values.
Results may differ from the reference program's by a relative error of at most 0.017.
Values may be sent and summed in bfloat16 or wider, within the bound.
A program may use at most 64 MiB of HBM per device.

```python
import jax
import jax.numpy as jnp
from jax import lax

D = 512
L = 2
BLK = 128
NB = 2
HB = 1
KT = 4
KC = 4
NBLOCKS = 32
NODES = 4096
N_GX = 16


def shared_counts(key):
    counts = jax.random.randint(key, (N_GX,), NB // 2, NB + 1, dtype=jnp.int32)
    counts = counts.at[0].set(NB)
    return counts.at[N_GX - 1].set(NB // 2)


def draw_block_count(key, part):
    counts = shared_counts(key)
    return counts


def draw_halo_list(key, part):
    counts = shared_counts(key)
    key = jax.random.fold_in(key, 11)
    raw_values = jax.random.randint(key, (N_GX, 2, HB), 0, 1 << 20, dtype=jnp.int32)
    chosen = raw_values % counts[:, None, None]
    chosen = chosen.at[0, 0, 0].set(NB - 1)
    return chosen.at[N_GX - 1, 1, 0].set(0)


def place_ends(values, own_key, low, top_value):
    longest = values.shape.index(max(values.shape))
    spots = []
    for shift in (0, 1):
        where = [jax.random.randint(jax.random.fold_in(own_key, axis), (), 0, length) for axis, length in enumerate(values.shape)]
        where[longest] = (where[longest] + shift) % values.shape[longest]
        spots.append(tuple(where))
    return values.at[spots[0]].set(low).at[spots[1]].set(top_value)


def shard_levels(key, shape, split, low, high):
    loudness = 1.0
    for dim, parts in split:
        heights = jax.random.uniform(jax.random.fold_in(jax.random.fold_in(key, 6), dim), (parts,), jnp.float32, low / len(split), high / len(split))
        loudness = loudness * jnp.repeat(jnp.exp(heights), shape[dim] // parts).reshape((-1,) + (1,) * (len(shape) - 1 - dim))
    return loudness


def gaussian(stream_key, extent, deviation, reach, split=(), kind=jnp.bfloat16):
    entries = deviation * jax.random.normal(stream_key, extent, jnp.float32)
    if split:
        entries = entries * shard_levels(stream_key, extent, split, -0.22, 0.18)
    return jnp.clip(entries, -reach, reach).astype(kind)


def setup_inputs(seed: int = 0, part: int = 0) -> dict:
    key_list = jax.random.split(jax.random.key(seed), 13)
    part_keys = jax.random.split(jax.random.fold_in(key_list[12], part), 13)
    node_feats = gaussian(part_keys[0], (NODES, D), 1.0, 6.0, ((0, 16),))
    cotangent = gaussian(part_keys[1], (NODES, D), 1.0, 6.0, ((0, 16),))
    tile_val = gaussian(part_keys[2], (NBLOCKS, KT, BLK, BLK), (KT * BLK) ** -0.5, 0.25, ((0, 16),))
    tile_src = place_ends(jax.random.randint(part_keys[3], (NBLOCKS, KT), 0, NB + 2 * HB), jax.random.fold_in(part_keys[3], 1), 0, (NB + 2 * HB) - 1).astype(jnp.int32)
    halo_list = draw_halo_list(jax.random.fold_in(jax.random.fold_in(key_list[12], part), 71), part)
    block_count = draw_block_count(jax.random.fold_in(jax.random.fold_in(key_list[12], part), 71), part)
    coarse_src = place_ends(jax.random.randint(part_keys[6], (NBLOCKS, KC), 0, 2 * NB), jax.random.fold_in(part_keys[6], 1), 0, (2 * NB) - 1).astype(jnp.int32)
    coarse_val = gaussian(part_keys[7], (NBLOCKS, KC), 0.5, 3.0, ((0, 16),), jnp.float32)
    w_self = gaussian(key_list[8], (L, D, D), D ** -0.5, 0.25)
    w_agg = gaussian(key_list[9], (L, D, D), D ** -0.5, 0.25)
    w_out = gaussian(key_list[10], (L, D, D), D ** -0.5, 0.25)
    norm_gain = jnp.clip(1.0 + 0.1 * jax.random.normal(key_list[11], (L, D), jnp.float32), 0.5, 1.5)
    return {"node_feats": node_feats, "cotangent": cotangent, "tile_val": tile_val, "tile_src": tile_src, "halo_list": halo_list, "block_count": block_count, "coarse_src": coarse_src, "coarse_val": coarse_val, "w_self": w_self, "w_agg": w_agg, "w_out": w_out, "norm_gain": norm_gain}


NORM_EPSILON = 1e-05

def exact_dot(left, right):
    return jnp.dot(left, right, precision=lax.Precision.HIGHEST)

def inner_rows(left, right):
    return lax.dot_general(left, right, (((0,), (0,)), ((), ())), preferred_element_type=jnp.float32)

def times_transpose(left, right):
    return lax.dot_general(left, right, (((1,), (1,)), ((), ())), preferred_element_type=jnp.float32)

def coarse_matrix(coarse_src, coarse_val, columns_count):
    columns = jnp.arange(columns_count, dtype=jnp.int32)
    onehot = (coarse_src[:, :, None] == columns[None, None, :]).astype(jnp.float32)
    return lax.optimization_barrier(jnp.sum(onehot * coarse_val[:, :, None], axis=1))

def node_update(current, agg_bf, self_weight, agg_weight, out_weight, gain_row, mask_rows):
    pre_act = jnp.dot(current, self_weight, preferred_element_type=jnp.float32)
    pre_act = pre_act + jnp.dot(agg_bf, agg_weight, preferred_element_type=jnp.float32)
    hidden = jax.nn.silu(pre_act).astype(jnp.bfloat16)
    lifted = jnp.dot(hidden, out_weight, preferred_element_type=jnp.float32)
    row_mean = lax.optimization_barrier(jnp.mean(lifted, axis=-1, keepdims=True))
    centred = lifted - row_mean
    inv_std = lax.rsqrt(lax.optimization_barrier(jnp.mean(centred * centred, axis=-1, keepdims=True)) + NORM_EPSILON)
    normed = centred * inv_std
    new_state = (mask_rows * (current.astype(jnp.float32) + normed * gain_row)).astype(jnp.bfloat16)
    return (new_state, (pre_act, hidden, normed, inv_std))

def node_backward(cotan, current, agg_bf, stored, self_weight, agg_weight, out_weight, gain_row, mask_rows):
    pre_act, hidden, normed, inv_std = stored
    masked = cotan * mask_rows
    gain_term = lax.optimization_barrier(jnp.sum(masked * normed, axis=0))
    scaled = masked * gain_row
    lifted_grad = inv_std * (scaled - lax.optimization_barrier(jnp.mean(scaled, axis=-1, keepdims=True)) - normed * lax.optimization_barrier(jnp.mean(scaled * normed, axis=-1, keepdims=True)))
    lifted_bf = lifted_grad.astype(jnp.bfloat16)
    out_term = inner_rows(hidden, lifted_bf)
    hidden_grad = times_transpose(lifted_bf, out_weight)
    sigmoid_pre = jax.nn.sigmoid(pre_act)
    pre_grad = (hidden_grad * sigmoid_pre * (1.0 + pre_act * (1.0 - sigmoid_pre))).astype(jnp.bfloat16)
    self_term = inner_rows(current, pre_grad)
    agg_term = inner_rows(agg_bf, pre_grad)
    state_grad = masked + times_transpose(pre_grad, self_weight)
    agg_grad = times_transpose(pre_grad, agg_weight).astype(jnp.bfloat16)
    return (state_grad, agg_grad, (self_term, agg_term, out_term, gain_term))

def aggregate(current, tiles, sources, halo_list, region_matrix):
    blocks = current.reshape(N_GX, NB, BLK, D)
    device_ids = jnp.arange(N_GX)[:, None, None]
    outgoing = blocks[device_ids, halo_list]
    zero_rim = jnp.zeros((1, HB, BLK, D), jnp.bfloat16)
    lower_rim = jnp.concatenate([zero_rim, outgoing[:-1, 1]], axis=0)
    upper_rim = jnp.concatenate([outgoing[1:, 0], zero_rim], axis=0)
    extended = jnp.concatenate([lower_rim, blocks, upper_rim], axis=1)

    def one_device(device_items):
        ext_dev, tile_dev, source_dev = device_items
        picked = ext_dev[source_dev]
        return jnp.einsum('bkij,bkjd->bid', tile_dev.astype(jnp.float32), picked.astype(jnp.float32))
    fine = lax.map(one_device, (extended, tiles, sources))
    region = blocks.reshape(N_GX // 2, 2 * NB, BLK * D).astype(jnp.float32)
    coarse = jnp.einsum('rds,rsf->rdf', region_matrix, region, precision=lax.Precision.HIGHEST)
    return (fine.reshape(-1, D) + coarse.reshape(-1, D)).astype(jnp.bfloat16)

def spread(agg_grad, tiles, sources, halo_list, region_matrix):
    grad_blocks = agg_grad.reshape(N_GX, NB, BLK, D)

    def one_back(device_items):
        tile_dev, source_dev, grad_dev = device_items
        contrib = jnp.einsum('bkij,bid->bkjd', tile_dev.astype(jnp.float32), grad_dev.astype(jnp.float32))
        zero_ext = jnp.zeros((NB + 2 * HB, BLK, D), jnp.float32)
        return zero_ext.at[source_dev.reshape(-1)].add(contrib.reshape(-1, BLK, D))
    ext_grad = lax.map(one_back, (tiles, sources, grad_blocks))
    local_grad = ext_grad[:, HB:HB + NB]
    lower_rim = ext_grad[:, :HB]
    upper_rim = ext_grad[:, HB + NB:]
    zero_rim = jnp.zeros((1, HB, BLK, D), jnp.float32)
    from_left = jnp.concatenate([zero_rim, upper_rim[:-1]], axis=0)
    from_right = jnp.concatenate([lower_rim[1:], zero_rim], axis=0)
    device_ids = jnp.arange(N_GX)[:, None]
    local_grad = local_grad.at[device_ids, halo_list[:, 0]].add(from_left)
    local_grad = local_grad.at[device_ids, halo_list[:, 1]].add(from_right)
    region = grad_blocks.reshape(N_GX // 2, 2 * NB, BLK * D).astype(jnp.float32)
    region_grad = jnp.einsum('rds,rdf->rsf', region_matrix, region, precision=lax.Precision.HIGHEST)
    return local_grad.reshape(-1, D) + region_grad.reshape(-1, D)

def reference(node_feats, cotangent, tile_val, tile_src, halo_list, block_count, coarse_src, coarse_val, w_self, w_agg, w_out, norm_gain):
    block_valid = (jnp.arange(NB)[None, :] < block_count[:, None]).astype(jnp.float32)
    mask_rows = jnp.broadcast_to(block_valid[:, :, None], (N_GX, NB, BLK)).reshape(-1, 1)
    region_matrix = coarse_matrix(coarse_src, coarse_val, 2 * NB).reshape(N_GX // 2, 2 * NB, 2 * NB)
    tiles = tile_val.reshape(N_GX, NB, KT, BLK, BLK)
    sources = tile_src.reshape(N_GX, NB, KT)
    current = node_feats * mask_rows.astype(jnp.bfloat16)
    stored_layers = []
    for layer_index in range(L):
        agg_bf = aggregate(current, tiles, sources, halo_list, region_matrix)
        new_state, stored = node_update(current, agg_bf, w_self[layer_index], w_agg[layer_index], w_out[layer_index], norm_gain[layer_index], mask_rows)
        stored_layers.append((current, agg_bf, stored))
        current = new_state
    cotan = cotangent.astype(jnp.float32)
    grad_terms = [None] * L
    for layer_index in reversed(range(L)):
        layer_input, agg_bf, stored = stored_layers[layer_index]
        state_grad, agg_grad, terms_here = node_backward(cotan, layer_input, agg_bf, stored, w_self[layer_index], w_agg[layer_index], w_out[layer_index], norm_gain[layer_index], mask_rows)
        cotan = state_grad + spread(agg_grad, tiles, sources, halo_list, region_matrix)
        grad_terms[layer_index] = terms_here
    feats_grad = (cotan * mask_rows).astype(jnp.bfloat16)
    self_grad = jnp.stack([item[0] for item in grad_terms]).astype(jnp.bfloat16)
    agg_grad_out = jnp.stack([item[1] for item in grad_terms]).astype(jnp.bfloat16)
    out_grad = jnp.stack([item[2] for item in grad_terms]).astype(jnp.bfloat16)
    gain_grad = jnp.stack([item[3] for item in grad_terms])
    return (current, feats_grad, self_grad, agg_grad_out, out_grad, gain_grad)
```

```python
import functools

import jax
import jax.numpy as jnp
from jax import lax
from jax.experimental import pallas as pl
from jax.experimental.pallas import tpu as pltpu
from jax.sharding import PartitionSpec as P

NORM_EPSILON = 1e-05
MESH = pl.DeviceIdType.MESH
F32 = jnp.float32
BF16 = jnp.bfloat16
ALIGN = 16


def dot(left, right, left_dim, right_dim):
    return lax.dot_general(
        left, right, (((left_dim,), (right_dim,)), ((), ())), preferred_element_type=F32
    )


def reduce_plan(rows, bits):
    plan = []
    for bit in bits:
        halves = rows % (2 * ALIGN) == 0
        if halves:
            rows //= 2
        plan.append((bit, rows, halves))
    return plan


def dim_orders(count):
    bits = []
    while 2 ** (len(bits) + 1) <= count:
        bits.append(len(bits))
    swapped = list(bits)
    if len(bits) >= 3:
        swapped[1], swapped[2] = swapped[2], swapped[1]
    return bits, swapped


class Sems:
    def __init__(self, ref):
        self.ref, self.used = ref, 0

    def take(self):
        self.used += 1
        return self.ref.at[self.used - 1]


def kernel(
    count,
    sem_count,
    tile_src,
    halo_list,
    block_count,
    coarse_src,
    coarse_val,
    feats_hbm,
    cotan_hbm,
    tiles_hbm,
    wself_hbm,
    wagg_hbm,
    wout_hbm,
    gain_vm,
    out_feats_hbm,
    feats_grad_hbm,
    self_grad_hbm,
    agg_grad_hbm,
    out_grad_hbm,
    gain_grad_vm,
    feats,
    cotan,
    tiles,
    wself,
    wagg,
    wout,
    adj,
    ext,
    halo_send,
    agg,
    pre,
    hidden,
    normed,
    inv_std,
    out_feats,
    feats_grad,
    back_send,
    back_recv,
    grads,
    red_send,
    red_recv,
    full,
    gain_send,
    gain_recv,
    sem_ref,
):
    sems = Sems(sem_ref)
    layers, width = gain_vm.shape
    nblocks, ktiles, blk, _ = tiles.shape
    rows = nblocks * blk
    slab = 3 * width

    me = lax.axis_index("gx")
    parity = me % 2
    sibling = me + 1 - 2 * parity
    across = me - 1 + 2 * parity
    other = (across + count) % count
    has_other = jnp.where(across == other, 1.0, 0.0).astype(F32)
    bits, swapped = dim_orders(count)

    def bit_of(bit):
        return (me // 2**bit) % 2

    def partner(bit):
        return me + (1 - 2 * bit_of(bit)) * 2**bit

    def local(src, dst):
        copy = pltpu.make_async_copy(src, dst, sems.take())
        copy.start()
        return copy

    def remote(src, dst, to):
        copy = pltpu.make_async_remote_copy(
            src_ref=src,
            dst_ref=dst,
            send_sem=sems.take(),
            recv_sem=sems.take(),
            device_id={"gx": to},
            device_id_type=MESH,
        )
        copy.start()
        return copy

    get_feats = local(feats_hbm, feats)
    get_tiles = local(tiles_hbm, tiles)
    get_wself = local(wself_hbm, wself)
    get_wagg = local(wagg_hbm, wagg)
    get_wout = local(wout_hbm, wout)
    get_cotan = local(cotan_hbm, cotan)

    barrier = pltpu.get_barrier_semaphore()
    peers = [partner(bit) for bit in bits] + [other]
    for peer in peers:
        pl.semaphore_signal(barrier, inc=1, device_id={"gx": peer}, device_id_type=MESH)

    row_ids = lax.broadcasted_iota(jnp.int32, (rows, 1), 0)
    mask = jnp.where(row_ids < block_count[0] * blk, 1.0, 0.0).astype(F32)
    halo_0, halo_1 = halo_list[0, 0, 0], halo_list[0, 1, 0]
    to_sibling = halo_1 + (halo_0 - halo_1) * parity
    to_other = halo_0 + (halo_1 - halo_0) * parity

    def hot(index, block):
        return jnp.where(index == block, 1.0, 0.0).astype(F32)

    def pick(ref, index):
        chosen = hot(index, 0) * ref[pl.ds(0, blk), :].astype(F32)
        for block in range(1, nblocks):
            chosen += hot(index, block) * ref[pl.ds(block * blk, blk), :].astype(F32)
        return chosen.astype(BF16)

    def start_halo(layer):
        here = ext.at[layer]
        halo_send[layer, pl.ds(0, blk), :] = pick(here, to_other)
        first = remote(
            halo_send.at[layer, pl.ds(0, blk)], ext.at[layer, pl.ds(rows, blk)], other
        )
        halo_send[layer, pl.ds(blk, blk), :] = pick(here, to_sibling)
        second = remote(
            ext.at[layer, pl.ds(0, rows)], ext.at[layer, pl.ds(rows + 2 * blk, rows)], sibling
        )
        third = remote(
            halo_send.at[layer, pl.ds(blk, blk)], ext.at[layer, pl.ds(rows + blk, blk)], sibling
        )
        return (first, second, third)

    get_feats.wait()
    ext[0, pl.ds(0, rows), :] = (feats[...].astype(F32) * mask).astype(BF16)
    pl.semaphore_wait(barrier, len(peers))
    halo = start_halo(0)

    get_tiles.wait()
    eye = (
        lax.broadcasted_iota(jnp.int32, (blk, blk), 0)
        == lax.broadcasted_iota(jnp.int32, (blk, blk), 1)
    )
    lower_at, upper_at = 0, nblocks + 1
    for d in range(nblocks):
        tile_f = [tiles[d, k].astype(F32) for k in range(ktiles)]
        srcs = [tile_src[d, k] for k in range(ktiles)]

        def tile_sum(slot, tile_f=tile_f, srcs=srcs):
            total = hot(srcs[0], slot) * tile_f[0]
            for k in range(1, ktiles):
                total += hot(srcs[k], slot) * tile_f[k]
            return total

        def link(column, d=d):
            total = hot(coarse_src[d, 0], column) * coarse_val[d, 0]
            for k in range(1, coarse_src.shape[1]):
                total += hot(coarse_src[d, k], column) * coarse_val[d, k]
            return total

        def put(value, column, d=d):
            adj[pl.ds(d * blk, blk), pl.ds(column * blk, blk)] = value.astype(BF16)

        for j in range(nblocks):
            own = link(nblocks * parity + j)
            put(tile_sum(1 + j) + jnp.where(eye, own, 0.0), j)
            theirs = link(nblocks * (1 - parity) + j)
            put(jnp.where(eye, theirs, 0.0), nblocks + 2 + j)
        other_slot = lower_at + (upper_at - lower_at) * parity
        put(has_other * tile_sum(other_slot), nblocks)
        put(tile_sum(upper_at + lower_at - other_slot), nblocks + 1)

    get_wself.wait()
    waiting = [get_wagg, get_wout]
    sig_grad = pre
    out_copy = None
    for layer in range(layers):
        own = ext[layer, pl.ds(0, rows), :]
        pre_self = dot(own, wself[layer], 1, 0)
        total = dot(adj[:, pl.ds(0, rows)], own, 1, 0)
        for copy in waiting:
            copy.wait()
        waiting = []
        for copy in halo:
            copy.wait()
        total += dot(
            adj[:, pl.ds(rows, rows + 2 * blk)], ext[layer, pl.ds(rows, rows + 2 * blk), :], 1, 0
        )
        agg_here = total.astype(BF16)
        agg[layer] = agg_here
        z = pre_self + dot(agg_here, wagg[layer], 1, 0)
        s = 1.0 / (1.0 + jnp.exp(-z))
        u = (z * s).astype(BF16)
        hidden[layer] = u
        y = dot(u, wout[layer], 1, 0)
        centred = y - jnp.mean(y, axis=-1, keepdims=True)
        inv = lax.rsqrt(jnp.mean(centred * centred, axis=-1, keepdims=True) + NORM_EPSILON)
        n = centred * inv
        new = (
            mask
            * (ext[layer, pl.ds(0, rows), :].astype(F32) + n * gain_vm[pl.ds(layer, 1), :])
        ).astype(BF16)
        if layer + 1 < layers:
            ext[layer + 1, pl.ds(0, rows), :] = new
            halo = start_halo(layer + 1)
        else:
            out_feats[...] = new
            out_copy = local(out_feats, out_feats_hbm)
        normed[layer] = n
        inv_std[layer] = inv
        sig_grad[layer] = s * (1.0 + z * (1.0 - s))

    half = slab // 2

    class Reducer:
        def __init__(self, layer, which, order):
            self.layer, self.which = layer, which
            self.plan = reduce_plan(half, order)
            self.off = which * half
            self.rows = half
            self.spots = []
            self.share = []
            at = 0
            for _, sent, halves in self.plan:
                self.spots.append(at)
                at += sent
            self.left = []

        def slot(self, ref, step):
            return ref.at[self.layer, self.which, pl.ds(self.spots[step], self.plan[step][1])]

        def at(self, off, size):
            return pl.ds(pl.multiple_of(off, ALIGN), size)

        def start(self, step):
            bit, size, halves = self.plan[step]
            away = self.off + (1 - bit_of(bit)) * size if halves else self.off
            src = self.slot(red_send, step)
            src[...] = grads[self.layer, self.at(away, size), :].astype(BF16)
            self.copy = remote(src, self.slot(red_recv, step), partner(bit))

        def finish(self, step):
            bit, size, halves = self.plan[step]
            self.copy.wait()
            came = self.slot(red_recv, step)[...].astype(F32)
            if halves:
                self.off = self.off + bit_of(bit) * size
                self.left.append((step, self.off, size))
                self.rows = size
                held = grads[self.layer, self.at(self.off, size), :]
            else:
                held = self.slot(red_send, step)[...].astype(F32)
            summed = held + came
            if step + 1 < len(self.plan):
                grads[self.layer, self.at(self.off, size), :] = summed
            else:
                full[self.layer, self.at(self.off, size), :] = summed.astype(BF16)

        def share_start(self):
            step, off, size = self.left.pop()
            region = full.at[self.layer, self.at(off, size)]
            self.copy = remote(region, region, partner(self.plan[step][0]))

        def share_finish(self):
            self.copy.wait()

    def flow(layer, gain_flow=None):
        parts = [Reducer(layer, 0, bits), Reducer(layer, 1, swapped)]
        steps = len(bits)
        for step in range(steps):
            for part in parts:
                part.start(step)
            if gain_flow is not None:
                gain_flow.start(step)
            yield
            for part in parts:
                part.finish(step)
            if gain_flow is not None:
                gain_flow.finish(step)
        while parts[0].left or parts[1].left:
            busy = [part for part in parts if part.left]
            for part in busy:
                part.share_start()
            yield
            for part in busy:
                part.share_finish()

    class Gains:
        def __init__(self, value):
            self.value = value

        def start(self, step):
            gain_send[step] = self.value
            self.copy = remote(gain_send.at[step], gain_recv.at[step], partner(bits[step]))

        def finish(self, step):
            self.copy.wait()
            self.value = self.value + gain_recv[step]

    flows = []

    def advance():
        for item in list(flows):
            try:
                next(item)
            except StopIteration:
                flows.remove(item)

    get_cotan.wait()
    grad = cotan[...].astype(F32)
    gain_rows = lax.broadcasted_iota(jnp.int32, gain_send.shape[1:], 0)
    gain_total = jnp.zeros(gain_send.shape[1:], F32)
    grad_copy = None
    for layer in reversed(range(layers)):
        n = normed[layer]
        masked = grad * mask
        scaled = masked * gain_vm[pl.ds(layer, 1), :]
        lifted = inv_std[layer] * (
            scaled
            - jnp.mean(scaled, axis=-1, keepdims=True)
            - n * jnp.mean(scaled * n, axis=-1, keepdims=True)
        )
        lifted = lifted.astype(BF16)
        back = dot(lifted, wout[layer], 1, 1)
        pre_grad = (back * sig_grad[layer]).astype(BF16)
        agg_back = dot(pre_grad, wagg[layer], 1, 1).astype(BF16)
        spread = dot(adj[:, pl.ds(rows, rows + 2 * blk)], agg_back, 0, 0)
        back_send[layer] = spread.astype(BF16)
        first = remote(
            back_send.at[layer, pl.ds(0, blk)], back_recv.at[layer, pl.ds(0, blk)], other
        )
        rest = pl.ds(blk, rows + blk)
        second = remote(back_send.at[layer, rest], back_recv.at[layer, rest], sibling)
        advance()
        gain_term = jnp.sum(masked * n, axis=0, keepdims=True)
        gain_total = jnp.where(gain_rows == layer, gain_term, gain_total)
        grads[layer, pl.ds(0, width), :] = dot(hidden[layer], lifted, 0, 0)
        grads[layer, pl.ds(width, width), :] = dot(ext[layer, pl.ds(0, rows), :], pre_grad, 0, 0)
        grads[layer, pl.ds(2 * width, width), :] = dot(agg[layer], pre_grad, 0, 0)
        gains = Gains(gain_total) if layer == 0 else None
        flows.append(flow(layer, gains))
        advance()
        grad = masked + dot(pre_grad, wself[layer], 1, 1)
        grad += dot(adj[:, pl.ds(0, rows)], agg_back, 0, 0)
        first.wait()
        second.wait()
        from_other = back_recv[layer, pl.ds(0, blk), :].astype(F32)
        from_sibling = back_recv[layer, pl.ds(blk, blk), :].astype(F32)
        pieces = [
            hot(to_other, j) * from_other + hot(to_sibling, j) * from_sibling
            for j in range(nblocks)
        ]
        grad += back_recv[layer, pl.ds(2 * blk, rows), :].astype(F32)
        grad += jnp.concatenate(pieces, axis=0)
        if layer > 0:
            advance()
    feats_grad[...] = (grad * mask).astype(BF16)
    grad_copy = local(feats_grad, feats_grad_hbm)
    while flows:
        advance()
    gain_grad_vm[...] = gains.value[0:layers]

    last = []
    for layer in range(layers):
        for part, target in enumerate((out_grad_hbm, self_grad_hbm, agg_grad_hbm)):
            last.append(local(full.at[layer, pl.ds(part * width, width)], target.at[layer]))
    for copy in last:
        copy.wait()
    out_copy.wait()
    grad_copy.wait()
    assert sems.used <= sem_count, sems.used


def per_device(
    count,
    node_feats,
    cotangent,
    tile_val,
    tile_src,
    halo_list,
    block_count,
    coarse_src,
    coarse_val,
    w_self,
    w_agg,
    w_out,
    norm_gain,
):
    rows, width = node_feats.shape
    nblocks, ktiles, blk, _ = tile_val.shape
    layers = w_self.shape[0]
    bits, _ = dim_orders(count)
    stages = len(bits)
    reduce_rows = sum(size for _, size, _ in reduce_plan(3 * width // 2, bits))
    sem_count = 32 + 10 * layers + 8 * layers * stages + 2 * stages + 4 * layers
    ext_rows = 2 * rows + 2 * blk
    any_space = pl.BlockSpec(memory_space=pl.ANY)
    smem = pl.BlockSpec(memory_space=pltpu.SMEM)
    vmem = pl.BlockSpec(memory_space=pltpu.VMEM)
    shape = jax.ShapeDtypeStruct
    weights = (layers, width, width)
    outs = pl.pallas_call(
        functools.partial(kernel, count, sem_count),
        out_shape=(
            shape((rows, width), BF16),
            shape((rows, width), BF16),
            shape(weights, BF16),
            shape(weights, BF16),
            shape(weights, BF16),
            shape((layers, width), F32),
        ),
        in_specs=[smem] * 5 + [any_space] * 6 + [vmem],
        out_specs=(any_space,) * 5 + (vmem,),
        scratch_shapes=[
            pltpu.VMEM((rows, width), BF16),
            pltpu.VMEM((rows, width), BF16),
            pltpu.VMEM(tile_val.shape, BF16),
            pltpu.VMEM(weights, BF16),
            pltpu.VMEM(weights, BF16),
            pltpu.VMEM(weights, BF16),
            pltpu.VMEM((rows, ext_rows), BF16),
            pltpu.VMEM((layers, ext_rows, width), BF16),
            pltpu.VMEM((layers, 2 * blk, width), BF16),
            pltpu.VMEM((layers, rows, width), BF16),
            pltpu.VMEM((layers, rows, width), F32),
            pltpu.VMEM((layers, rows, width), BF16),
            pltpu.VMEM((layers, rows, width), F32),
            pltpu.VMEM((layers, rows, 1), F32),
            pltpu.VMEM((rows, width), BF16),
            pltpu.VMEM((rows, width), BF16),
            pltpu.VMEM((layers, rows + 2 * blk, width), BF16),
            pltpu.VMEM((layers, rows + 2 * blk, width), BF16),
            pltpu.VMEM((layers, 3 * width, width), F32),
            pltpu.VMEM((layers, 2, reduce_rows, width), BF16),
            pltpu.VMEM((layers, 2, reduce_rows, width), BF16),
            pltpu.VMEM((layers, 3 * width, width), BF16),
            pltpu.VMEM((stages, 8, width), F32),
            pltpu.VMEM((stages, 8, width), F32),
            pltpu.SemaphoreType.DMA((sem_count,)),
        ],
        compiler_params=pltpu.CompilerParams(
            collective_id=0, has_side_effects=True, vmem_limit_bytes=50 * 2**20
        ),
        cost_estimate=pl.CostEstimate(
            flops=3 * 10**9, bytes_accessed=10 * 2**20, transcendentals=2 * layers * rows * width
        ),
    )(
        tile_src,
        halo_list,
        block_count,
        coarse_src,
        coarse_val,
        node_feats,
        cotangent,
        tile_val,
        w_self,
        w_agg,
        w_out,
        norm_gain,
    )
    return tuple(outs)


def solution(mesh):
    nodes = P(("groups", "gx"), None)
    return jax.shard_map(
        functools.partial(per_device, mesh.shape["gx"]),
        mesh=mesh,
        in_specs=(
            nodes,
            nodes,
            P(("groups", "gx"), None, None, None),
            nodes,
            P(("groups", "gx"), None, None),
            P(("groups", "gx")),
            nodes,
            nodes,
            P(),
            P(),
            P(),
            P(),
        ),
        out_specs=(
            nodes,
            nodes,
            P("groups", None, None),
            P("groups", None, None),
            P("groups", None, None),
            P("groups", None),
        ),
        check_vma=False,
    )
```

```python
import functools

import jax
import jax.numpy as jnp
from jax import lax
from jax.experimental import pallas as pl
from jax.experimental.pallas import tpu as pltpu
from jax.sharding import PartitionSpec as P

NORM_EPSILON = 1e-05
MESH = pl.DeviceIdType.MESH
F32 = jnp.float32
BF16 = jnp.bfloat16
ALIGN = 16


def dot(left, right, left_dim, right_dim):
    return lax.dot_general(
        left, right, (((left_dim,), (right_dim,)), ((), ())), preferred_element_type=F32
    )


def reduce_plan(rows, groups):
    plan = []
    for bit, size in groups:
        split = rows % (size * ALIGN) == 0
        if split:
            rows //= size
        plan.append((bit, size, rows, split))
    return plan


def slot_rows(plan):
    return sum((size - 1) * rows for _, size, rows, _ in plan)


def group_orders(count):
    groups, bit = [], 0
    while 2**bit < count:
        groups.append((bit, 2))
        bit += 1
    swapped = list(groups)
    if len(groups) >= 3:
        swapped[1], swapped[2] = swapped[2], swapped[1]
    return groups, swapped, groups


def part_rows(width):
    return (width, width, width)


class Sems:
    def __init__(self, ref):
        self.ref, self.used = ref, 0

    def take(self):
        self.used += 1
        return self.ref.at[self.used - 1]


def kernel(
    count,
    sem_count,
    tile_src,
    halo_list,
    block_count,
    coarse_src,
    coarse_val,
    feats_hbm,
    cotan_hbm,
    tiles_hbm,
    wself_hbm,
    wagg_hbm,
    wout_hbm,
    gain_vm,
    out_feats_hbm,
    feats_grad_hbm,
    self_grad_hbm,
    agg_grad_hbm,
    out_grad_hbm,
    gain_grad_vm,
    feats,
    cotan,
    tiles,
    wself,
    wagg,
    wout,
    adj,
    ext,
    halo_send,
    agg,
    pre,
    hidden,
    normed,
    inv_std,
    out_feats,
    feats_grad,
    back_send,
    back_recv,
    grads,
    red_send,
    red_recv,
    full,
    gain_send,
    gain_recv,
    sem_ref,
):
    sems = Sems(sem_ref)
    layers, width = gain_vm.shape
    nblocks, ktiles, blk, _ = tiles.shape
    rows = nblocks * blk
    slab = 3 * width

    me = lax.axis_index("gx")
    parity = me % 2
    sibling = me + 1 - 2 * parity
    across = me - 1 + 2 * parity
    other = (across + count) % count
    has_other = jnp.where(across == other, 1.0, 0.0).astype(F32)
    orders = group_orders(count)

    def place(bit, size):
        return (me // 2**bit) % size

    def peer(bit, size, by):
        mine = place(bit, size)
        return me + ((mine + by) % size - mine) * 2**bit

    def local(src, dst):
        copy = pltpu.make_async_copy(src, dst, sems.take())
        copy.start()
        return copy

    class AcrossCopy:
        def __init__(self, src, dst):
            self.copy = remote(src, dst, other, start=False)

            @pl.when(across == other)
            def _():
                self.copy.start()

            @pl.when(across != other)
            def _():
                dst[...] = jnp.zeros(dst.shape, dst.dtype)

        def wait(self):
            @pl.when(across == other)
            def _():
                self.copy.wait()

    def remote(src, dst, to, start=True):
        copy = pltpu.make_async_remote_copy(
            src_ref=src,
            dst_ref=dst,
            send_sem=sems.take(),
            recv_sem=sems.take(),
            device_id={"gx": to},
            device_id_type=MESH,
        )
        if start:
            copy.start()
        return copy

    get_feats = local(feats_hbm, feats)
    get_tiles = local(tiles_hbm, tiles)
    get_wself = local(wself_hbm, wself)
    get_wagg = local(wagg_hbm, wagg)
    get_wout = local(wout_hbm, wout)
    get_cotan = local(cotan_hbm, cotan)

    barrier = pltpu.get_barrier_semaphore()
    peers = [peer(bit, size, by) for bit, size in orders[0] for by in range(1, size)] + [other]
    for to in peers:
        pl.semaphore_signal(barrier, inc=1, device_id={"gx": to}, device_id_type=MESH)

    row_ids = lax.broadcasted_iota(jnp.int32, (rows, 1), 0)
    mask = jnp.where(row_ids < block_count[0] * blk, 1.0, 0.0).astype(F32)
    halo_0, halo_1 = halo_list[0, 0, 0], halo_list[0, 1, 0]
    to_sibling = halo_1 + (halo_0 - halo_1) * parity
    to_other = halo_0 + (halo_1 - halo_0) * parity

    def hot(index, block):
        return jnp.where(index == block, 1.0, 0.0).astype(F32)

    def pick(ref, index):
        chosen = hot(index, 0) * ref[pl.ds(0, blk), :].astype(F32)
        for block in range(1, nblocks):
            chosen += hot(index, block) * ref[pl.ds(block * blk, blk), :].astype(F32)
        return chosen.astype(BF16)

    def start_halo(layer):
        here = ext.at[layer]
        halo_send[layer, pl.ds(0, blk), :] = pick(here, to_other)
        first = AcrossCopy(
            halo_send.at[layer, pl.ds(0, blk)], ext.at[layer, pl.ds(rows, blk)]
        )
        halo_send[layer, pl.ds(blk, blk), :] = pick(here, to_sibling)
        second = remote(
            ext.at[layer, pl.ds(0, rows)], ext.at[layer, pl.ds(rows + 2 * blk, rows)], sibling
        )
        third = remote(
            halo_send.at[layer, pl.ds(blk, blk)], ext.at[layer, pl.ds(rows + blk, blk)], sibling
        )
        return (first, second, third)

    get_feats.wait()
    ext[0, pl.ds(0, rows), :] = (feats[...].astype(F32) * mask).astype(BF16)
    pl.semaphore_wait(barrier, len(peers))
    halo = start_halo(0)

    get_tiles.wait()
    eye = (
        lax.broadcasted_iota(jnp.int32, (blk, blk), 0)
        == lax.broadcasted_iota(jnp.int32, (blk, blk), 1)
    )
    lower_at, upper_at = 0, nblocks + 1
    for d in range(nblocks):
        tile_f = [tiles[d, k].astype(F32) for k in range(ktiles)]
        srcs = [tile_src[d, k] for k in range(ktiles)]

        def tile_sum(slot, tile_f=tile_f, srcs=srcs):
            total = hot(srcs[0], slot) * tile_f[0]
            for k in range(1, ktiles):
                total += hot(srcs[k], slot) * tile_f[k]
            return total

        def link(column, d=d):
            total = hot(coarse_src[d, 0], column) * coarse_val[d, 0]
            for k in range(1, coarse_src.shape[1]):
                total += hot(coarse_src[d, k], column) * coarse_val[d, k]
            return total

        def put(value, column, d=d):
            adj[pl.ds(d * blk, blk), pl.ds(column * blk, blk)] = value.astype(BF16)

        for j in range(nblocks):
            own = link(nblocks * parity + j)
            put(tile_sum(1 + j) + jnp.where(eye, own, 0.0), j)
            theirs = link(nblocks * (1 - parity) + j)
            put(jnp.where(eye, theirs, 0.0), nblocks + 2 + j)
        other_slot = lower_at + (upper_at - lower_at) * parity
        put(has_other * tile_sum(other_slot), nblocks)
        put(tile_sum(upper_at + lower_at - other_slot), nblocks + 1)

    get_wself.wait()
    waiting = [get_wagg, get_wout]
    sig_grad = pre
    out_copy = None
    for layer in range(layers):
        own = ext[layer, pl.ds(0, rows), :]
        pre_self = dot(own, wself[layer], 1, 0)
        total = dot(adj[:, pl.ds(0, rows)], own, 1, 0)
        for copy in waiting:
            copy.wait()
        waiting = []
        for copy in halo:
            copy.wait()
        total += dot(
            adj[:, pl.ds(rows, rows + 2 * blk)], ext[layer, pl.ds(rows, rows + 2 * blk), :], 1, 0
        )
        agg_here = total.astype(BF16)
        agg[layer] = agg_here
        z = pre_self + dot(agg_here, wagg[layer], 1, 0)
        s = 1.0 / (1.0 + jnp.exp(-z))
        u = (z * s).astype(BF16)
        hidden[layer] = u
        y = dot(u, wout[layer], 1, 0)
        centred = y - jnp.mean(y, axis=-1, keepdims=True)
        inv = lax.rsqrt(jnp.mean(centred * centred, axis=-1, keepdims=True) + NORM_EPSILON)
        n = centred * inv
        new = (
            mask
            * (ext[layer, pl.ds(0, rows), :].astype(F32) + n * gain_vm[pl.ds(layer, 1), :])
        ).astype(BF16)
        if layer + 1 < layers:
            ext[layer + 1, pl.ds(0, rows), :] = new
            halo = start_halo(layer + 1)
        else:
            out_feats[...] = new
            out_copy = local(out_feats, out_feats_hbm)
        normed[layer] = n
        inv_std[layer] = inv
        sig_grad[layer] = s * (1.0 + z * (1.0 - s))

    class Reducer:
        def __init__(self, layer, which, gains=None):
            self.layer, self.which, self.gains = layer, which, gains
            parts = part_rows(width)
            self.plan = reduce_plan(parts[which], orders[which])
            self.off = sum(parts[:which])
            self.base = sum(slot_rows(reduce_plan(parts[i], orders[i])) for i in range(which))
            self.left = []

        def slot(self, ref, step, by):
            at = self.base + slot_rows(self.plan[:step]) + (by - 1) * self.plan[step][2]
            return ref.at[self.layer, pl.ds(at, self.plan[step][2])]

        def at(self, off, size):
            return pl.ds(pl.multiple_of(off, ALIGN), size)

        def start(self, step):
            bit, size, share, split = self.plan[step]
            mine = place(bit, size)
            self.copies = []
            for by in range(1, size):
                away = self.off + (mine + by) % size * share if split else self.off
                src = self.slot(red_send, step, by)
                src[...] = grads[self.layer, self.at(away, share), :].astype(BF16)
                self.copies.append(remote(src, self.slot(red_recv, step, by), peer(bit, size, by)))
            if self.gains is not None:
                self.gains.start(step)

        def finish(self, step):
            bit, size, share, split = self.plan[step]
            if split:
                self.off = self.off + place(bit, size) * share
                self.left.append((bit, size, self.off, share))
                summed = grads[self.layer, self.at(self.off, share), :]
            else:
                summed = self.slot(red_send, step, 1)[...].astype(F32)
            for copy in self.copies:
                copy.wait()
            for by in range(1, size):
                summed = summed + self.slot(red_recv, step, by)[...].astype(F32)
            if step + 1 < len(self.plan):
                grads[self.layer, self.at(self.off, share), :] = summed
            else:
                full[self.layer, self.at(self.off, share), :] = summed.astype(BF16)
            if self.gains is not None:
                self.gains.finish(step)

        def flow(self):
            for step in range(len(self.plan)):
                self.start(step)
                yield
                self.finish(step)
            for bit, size, off, share in reversed(self.left):
                region = full.at[self.layer, self.at(off, share)]
                copies = [remote(region, region, peer(bit, size, by)) for by in range(1, size)]
                yield
                for copy in copies:
                    copy.wait()

    class Gains:
        def __init__(self, value):
            self.value, self.used = value, 0

        def start(self, step):
            bit, size = orders[0][step]
            self.copies = []
            self.slots = range(self.used, self.used + size - 1)
            self.used += size - 1
            gain_send[step] = self.value
            for by, slot in enumerate(self.slots, 1):
                self.copies.append(
                    remote(gain_send.at[step], gain_recv.at[slot], peer(bit, size, by))
                )

        def finish(self, step):
            bit, size = orders[0][step]
            for copy in self.copies:
                copy.wait()
            if size == 2:
                self.value = self.value + gain_recv[self.slots[0]]
                return
            mine = place(bit, size)
            terms = [self.value] + [gain_recv[slot] for slot in self.slots]
            total = jnp.zeros_like(self.value)
            for want in range(size):
                for by in range(size):
                    total = total + jnp.where((mine - by + size) % size == want, 1.0, 0.0) * terms[by]
            self.value = total

    flows = []

    def advance():
        for item in list(flows):
            try:
                next(item)
            except StopIteration:
                flows.remove(item)

    gains = None

    def begin(layer, which, left, right):
        grads[layer, pl.ds(which * width, width), :] = dot(left, right, 0, 0)
        last = gains if layer == 0 and which == 2 else None
        flows.append(Reducer(layer, which, last).flow())
        next(flows[-1])

    get_cotan.wait()
    grad = cotan[...].astype(F32)
    gain_rows = lax.broadcasted_iota(jnp.int32, gain_send.shape[1:], 0)
    gain_total = jnp.zeros(gain_send.shape[1:], F32)
    grad_copy = None
    for layer in reversed(range(layers)):
        n = normed[layer]
        masked = grad * mask
        scaled = masked * gain_vm[pl.ds(layer, 1), :]
        lifted = inv_std[layer] * (
            scaled
            - jnp.mean(scaled, axis=-1, keepdims=True)
            - n * jnp.mean(scaled * n, axis=-1, keepdims=True)
        )
        lifted = lifted.astype(BF16)
        if layer == 0:
            begin(layer, 0, hidden[layer], lifted)
        back = dot(lifted, wout[layer], 1, 1)
        pre_grad = (back * sig_grad[layer]).astype(BF16)
        gain_term = jnp.sum(masked * n, axis=0, keepdims=True)
        gain_total = jnp.where(gain_rows == layer, gain_term, gain_total)
        if layer == 0:
            gains = Gains(gain_total)
            begin(layer, 1, ext[layer, pl.ds(0, rows), :], pre_grad)
            begin(layer, 2, agg[layer], pre_grad)
        agg_back = dot(pre_grad, wagg[layer], 1, 1).astype(BF16)
        spread = dot(adj[:, pl.ds(rows, rows + 2 * blk)], agg_back, 0, 0)
        back_send[layer] = spread.astype(BF16)
        first = AcrossCopy(
            back_send.at[layer, pl.ds(0, blk)], back_recv.at[layer, pl.ds(0, blk)]
        )
        rest = pl.ds(blk, rows + blk)
        second = remote(back_send.at[layer, rest], back_recv.at[layer, rest], sibling)
        if layer > 0:
            begin(layer, 0, hidden[layer], lifted)
            begin(layer, 1, ext[layer, pl.ds(0, rows), :], pre_grad)
            begin(layer, 2, agg[layer], pre_grad)
        grad = masked + dot(pre_grad, wself[layer], 1, 1)
        grad += dot(adj[:, pl.ds(0, rows)], agg_back, 0, 0)
        advance()
        first.wait()
        second.wait()
        from_other = back_recv[layer, pl.ds(0, blk), :].astype(F32)
        from_sibling = back_recv[layer, pl.ds(blk, blk), :].astype(F32)
        pieces = [
            hot(to_other, j) * from_other + hot(to_sibling, j) * from_sibling
            for j in range(nblocks)
        ]
        grad += back_recv[layer, pl.ds(2 * blk, rows), :].astype(F32)
        grad += jnp.concatenate(pieces, axis=0)
    feats_grad[...] = (grad * mask).astype(BF16)
    grad_copy = local(feats_grad, feats_grad_hbm)
    while flows:
        advance()
    gain_grad_vm[...] = gains.value[0:layers]

    last = []
    for layer in range(layers):
        for part, target in enumerate((out_grad_hbm, self_grad_hbm, agg_grad_hbm)):
            last.append(local(full.at[layer, pl.ds(part * width, width)], target.at[layer]))
    for copy in last:
        copy.wait()
    out_copy.wait()
    grad_copy.wait()
    assert sems.used <= sem_count, sems.used


def copy_kernel(*refs):
    count = len(refs) // 3
    sources, targets, stages, sem = refs[:count], refs[count : 2 * count], refs[2 * count : -1], refs[-1]
    loads, stores = [], []
    for i in range(count):
        loads.append(pltpu.make_async_copy(sources[i], stages[i], sem.at[0, i]))
        loads[-1].start()
    for i in range(count):
        loads[i].wait()
        stores.append(pltpu.make_async_copy(stages[i], targets[i], sem.at[1, i]))
        stores[-1].start()
    for store in stores:
        store.wait()


def copied_out(arrays):
    return pl.pallas_call(
        copy_kernel,
        out_shape=tuple(jax.ShapeDtypeStruct(x.shape, x.dtype) for x in arrays),
        in_specs=[pl.BlockSpec(memory_space=pl.ANY)] * len(arrays),
        out_specs=(pl.BlockSpec(memory_space=pl.ANY),) * len(arrays),
        scratch_shapes=[pltpu.VMEM(x.shape, x.dtype) for x in arrays]
        + [pltpu.SemaphoreType.DMA((2, len(arrays)))],
    )(*arrays)


def per_device(
    count,
    node_feats,
    cotangent,
    tile_val,
    tile_src,
    halo_list,
    block_count,
    coarse_src,
    coarse_val,
    w_self,
    w_agg,
    w_out,
    norm_gain,
):
    rows, width = node_feats.shape
    nblocks, ktiles, blk, _ = tile_val.shape
    layers = w_self.shape[0]
    orders = group_orders(count)
    stages = len(orders[0])
    links = sum(size - 1 for _, size in orders[0])
    plans = [reduce_plan(rows, order) for rows, order in zip(part_rows(width), orders)]
    reduce_rows = sum(slot_rows(plan) for plan in plans)
    sem_count = 32 + 14 * layers + 4 * len(plans) * layers * links + 2 * links
    ext_rows = 2 * rows + 2 * blk
    any_space = pl.BlockSpec(memory_space=pl.ANY)
    smem = pl.BlockSpec(memory_space=pltpu.SMEM)
    vmem = pl.BlockSpec(memory_space=pltpu.VMEM)
    shape = jax.ShapeDtypeStruct
    weights = (layers, width, width)
    outs = pl.pallas_call(
        functools.partial(kernel, count, sem_count),
        out_shape=(
            shape((rows, width), BF16),
            shape((rows, width), BF16),
            shape(weights, BF16),
            shape(weights, BF16),
            shape(weights, BF16),
            shape((layers, width), F32),
        ),
        in_specs=[smem] * 5 + [any_space] * 6 + [vmem],
        out_specs=(any_space,) * 5 + (vmem,),
        scratch_shapes=[
            pltpu.VMEM((rows, width), BF16),
            pltpu.VMEM((rows, width), BF16),
            pltpu.VMEM(tile_val.shape, BF16),
            pltpu.VMEM(weights, BF16),
            pltpu.VMEM(weights, BF16),
            pltpu.VMEM(weights, BF16),
            pltpu.VMEM((rows, ext_rows), BF16),
            pltpu.VMEM((layers, ext_rows, width), BF16),
            pltpu.VMEM((layers, 2 * blk, width), BF16),
            pltpu.VMEM((layers, rows, width), BF16),
            pltpu.VMEM((layers, rows, width), F32),
            pltpu.VMEM((layers, rows, width), BF16),
            pltpu.VMEM((layers, rows, width), F32),
            pltpu.VMEM((layers, rows, 1), F32),
            pltpu.VMEM((rows, width), BF16),
            pltpu.VMEM((rows, width), BF16),
            pltpu.VMEM((layers, rows + 2 * blk, width), BF16),
            pltpu.VMEM((layers, rows + 2 * blk, width), BF16),
            pltpu.VMEM((layers, 3 * width, width), F32),
            pltpu.VMEM((layers, reduce_rows, width), BF16),
            pltpu.VMEM((layers, reduce_rows, width), BF16),
            pltpu.VMEM((layers, 3 * width, width), BF16),
            pltpu.VMEM((stages, 8, width), F32),
            pltpu.VMEM((links, 8, width), F32),
            pltpu.SemaphoreType.DMA((sem_count,)),
        ],
        compiler_params=pltpu.CompilerParams(
            collective_id=0, has_side_effects=True, vmem_limit_bytes=63 * 2**20
        ),
        cost_estimate=pl.CostEstimate(
            flops=3 * 10**9, bytes_accessed=10 * 2**20, transcendentals=2 * layers * rows * width
        ),
    )(
        tile_src,
        halo_list,
        block_count,
        coarse_src,
        coarse_val,
        node_feats,
        cotangent,
        tile_val,
        w_self,
        w_agg,
        w_out,
        norm_gain,
    )
    return copied_out(outs)


def solution(mesh):
    nodes = P(("groups", "gx"), None)
    return jax.shard_map(
        functools.partial(per_device, mesh.shape["gx"]),
        mesh=mesh,
        in_specs=(
            nodes,
            nodes,
            P(("groups", "gx"), None, None, None),
            nodes,
            P(("groups", "gx"), None, None),
            P(("groups", "gx")),
            nodes,
            nodes,
            P(),
            P(),
            P(),
            P(),
        ),
        out_specs=(
            nodes,
            nodes,
            P("groups", None, None),
            P("groups", None, None),
            P("groups", None, None),
            P("groups", None),
        ),
        check_vma=False,
    )
```

```python
import functools

import jax
import jax.numpy as jnp
from jax import lax
from jax.experimental import pallas as pl
from jax.experimental.pallas import tpu as pltpu
from jax.sharding import PartitionSpec as P

NORM_EPSILON = 1e-05
MESH = pl.DeviceIdType.MESH
F32 = jnp.float32
BF16 = jnp.bfloat16
ALIGN = 16


def dot(left, right, left_dim, right_dim):
    return lax.dot_general(
        left, right, (((left_dim,), (right_dim,)), ((), ())), preferred_element_type=F32
    )


def reduce_plan(rows, groups):
    plan = []
    for bit, size in groups:
        split = rows % (size * ALIGN) == 0
        if split:
            rows //= size
        plan.append((bit, size, rows, split))
    return plan


def slot_rows(plan):
    return sum((size - 1) * rows for _, size, rows, _ in plan)


def group_orders(count):
    groups, bit = [], 0
    while 2**bit < count:
        groups.append((bit, 2))
        bit += 1
    swapped = list(groups)
    if len(groups) >= 3:
        swapped[1], swapped[2] = swapped[2], swapped[1]
    return groups, swapped, groups


def part_rows(width):
    return (width, width, width)


class Sems:
    def __init__(self, ref):
        self.ref, self.used = ref, 0

    def take(self):
        self.used += 1
        return self.ref.at[self.used - 1]


def kernel(
    count,
    sem_count,
    tile_src,
    halo_list,
    block_count,
    coarse_src,
    coarse_val,
    feats_hbm,
    cotan_hbm,
    tiles_hbm,
    wself_hbm,
    wagg_hbm,
    wout_hbm,
    gain_vm,
    out_feats_hbm,
    feats_grad_hbm,
    self_grad_hbm,
    agg_grad_hbm,
    out_grad_hbm,
    gain_grad_vm,
    feats,
    cotan,
    tiles,
    wself,
    wagg,
    wout,
    adj,
    ext,
    halo_send,
    agg,
    pre,
    hidden,
    normed,
    inv_std,
    out_feats,
    feats_grad,
    back_send,
    back_recv,
    grads,
    red_send,
    red_recv,
    full,
    gain_send,
    gain_recv,
    sem_ref,
):
    sems = Sems(sem_ref)
    layers, width = gain_vm.shape
    nblocks, ktiles, blk, _ = tiles.shape
    rows = nblocks * blk
    slab = 3 * width

    me = lax.axis_index("gx")
    parity = me % 2
    sibling = me + 1 - 2 * parity
    across = me - 1 + 2 * parity
    other = (across + count) % count
    has_other = jnp.where(across == other, 1.0, 0.0).astype(F32)
    orders = group_orders(count)

    def place(bit, size):
        return (me // 2**bit) % size

    def peer(bit, size, by):
        mine = place(bit, size)
        return me + ((mine + by) % size - mine) * 2**bit

    def local(src, dst):
        copy = pltpu.make_async_copy(src, dst, sems.take())
        copy.start()
        return copy

    class AcrossCopy:
        def __init__(self, src, dst):
            self.copy = remote(src, dst, other, start=False)

            @pl.when(across == other)
            def _():
                self.copy.start()

            @pl.when(across != other)
            def _():
                dst[...] = jnp.zeros(dst.shape, dst.dtype)

        def wait(self):
            @pl.when(across == other)
            def _():
                self.copy.wait()

    def remote(src, dst, to, start=True):
        copy = pltpu.make_async_remote_copy(
            src_ref=src,
            dst_ref=dst,
            send_sem=sems.take(),
            recv_sem=sems.take(),
            device_id={"gx": to},
            device_id_type=MESH,
        )
        if start:
            copy.start()
        return copy

    get_feats = local(feats_hbm, feats)
    get_tiles = local(tiles_hbm, tiles)
    get_wself = local(wself_hbm, wself)
    get_wagg = local(wagg_hbm, wagg)
    get_wout = local(wout_hbm, wout)
    get_cotan = local(cotan_hbm, cotan)

    barrier = pltpu.get_barrier_semaphore()
    peers = [peer(bit, size, by) for bit, size in orders[0] for by in range(1, size)] + [other]
    for to in peers:
        pl.semaphore_signal(barrier, inc=1, device_id={"gx": to}, device_id_type=MESH)

    row_ids = lax.broadcasted_iota(jnp.int32, (rows, 1), 0)
    mask = jnp.where(row_ids < block_count[0] * blk, 1.0, 0.0).astype(F32)
    halo_0, halo_1 = halo_list[0, 0, 0], halo_list[0, 1, 0]
    to_sibling = halo_1 + (halo_0 - halo_1) * parity
    to_other = halo_0 + (halo_1 - halo_0) * parity

    def hot(index, block):
        return jnp.where(index == block, 1.0, 0.0).astype(F32)

    def pick(ref, index):
        chosen = hot(index, 0) * ref[pl.ds(0, blk), :].astype(F32)
        for block in range(1, nblocks):
            chosen += hot(index, block) * ref[pl.ds(block * blk, blk), :].astype(F32)
        return chosen.astype(BF16)

    def start_halo(layer):
        here = ext.at[layer]
        halo_send[layer, pl.ds(0, blk), :] = pick(here, to_other)
        first = AcrossCopy(
            halo_send.at[layer, pl.ds(0, blk)], ext.at[layer, pl.ds(rows, blk)]
        )
        halo_send[layer, pl.ds(blk, blk), :] = pick(here, to_sibling)
        second = remote(
            ext.at[layer, pl.ds(0, rows)], ext.at[layer, pl.ds(rows + 2 * blk, rows)], sibling
        )
        third = remote(
            halo_send.at[layer, pl.ds(blk, blk)], ext.at[layer, pl.ds(rows + blk, blk)], sibling
        )
        return (first, second, third)

    get_feats.wait()
    ext[0, pl.ds(0, rows), :] = (feats[...].astype(F32) * mask).astype(BF16)
    pl.semaphore_wait(barrier, len(peers))
    halo = start_halo(0)

    get_tiles.wait()
    eye = (
        lax.broadcasted_iota(jnp.int32, (blk, blk), 0)
        == lax.broadcasted_iota(jnp.int32, (blk, blk), 1)
    )
    lower_at, upper_at = 0, nblocks + 1
    for d in range(nblocks):
        tile_f = [tiles[d, k].astype(F32) for k in range(ktiles)]
        srcs = [tile_src[d, k] for k in range(ktiles)]

        def tile_sum(slot, tile_f=tile_f, srcs=srcs):
            total = hot(srcs[0], slot) * tile_f[0]
            for k in range(1, ktiles):
                total += hot(srcs[k], slot) * tile_f[k]
            return total

        def link(column, d=d):
            total = hot(coarse_src[d, 0], column) * coarse_val[d, 0]
            for k in range(1, coarse_src.shape[1]):
                total += hot(coarse_src[d, k], column) * coarse_val[d, k]
            return total

        def put(value, column, d=d):
            adj[pl.ds(d * blk, blk), pl.ds(column * blk, blk)] = value.astype(BF16)

        for j in range(nblocks):
            own = link(nblocks * parity + j)
            put(tile_sum(1 + j) + jnp.where(eye, own, 0.0), j)
            theirs = link(nblocks * (1 - parity) + j)
            put(jnp.where(eye, theirs, 0.0), nblocks + 2 + j)
        other_slot = lower_at + (upper_at - lower_at) * parity
        put(has_other * tile_sum(other_slot), nblocks)
        put(tile_sum(upper_at + lower_at - other_slot), nblocks + 1)

    get_wself.wait()
    waiting = [get_wagg, get_wout]
    sig_grad = pre
    out_copy = None
    for layer in range(layers):
        own = ext[layer, pl.ds(0, rows), :]
        pre_self = dot(own, wself[layer], 1, 0)
        total = dot(adj[:, pl.ds(0, rows)], own, 1, 0)
        for copy in waiting:
            copy.wait()
        waiting = []
        for copy in halo:
            copy.wait()
        total += dot(
            adj[:, pl.ds(rows, rows + 2 * blk)], ext[layer, pl.ds(rows, rows + 2 * blk), :], 1, 0
        )
        agg_here = total.astype(BF16)
        agg[layer] = agg_here
        z = pre_self + dot(agg_here, wagg[layer], 1, 0)
        s = 1.0 / (1.0 + jnp.exp(-z))
        u = (z * s).astype(BF16)
        hidden[layer] = u
        y = dot(u, wout[layer], 1, 0)
        centred = y - jnp.mean(y, axis=-1, keepdims=True)
        inv = lax.rsqrt(jnp.mean(centred * centred, axis=-1, keepdims=True) + NORM_EPSILON)
        n = centred * inv
        new = (
            mask
            * (ext[layer, pl.ds(0, rows), :].astype(F32) + n * gain_vm[pl.ds(layer, 1), :])
        ).astype(BF16)
        if layer + 1 < layers:
            ext[layer + 1, pl.ds(0, rows), :] = new
            halo = start_halo(layer + 1)
        else:
            out_feats[...] = new
            out_copy = local(out_feats, out_feats_hbm)
        normed[layer] = n
        inv_std[layer] = inv
        sig_grad[layer] = s * (1.0 + z * (1.0 - s))

    class Reducer:
        def __init__(self, layer, which, gains=None):
            self.layer, self.which, self.gains = layer, which, gains
            parts = part_rows(width)
            self.plan = reduce_plan(parts[which], orders[which])
            self.off = sum(parts[:which])
            self.base = sum(slot_rows(reduce_plan(parts[i], orders[i])) for i in range(which))
            self.left = []

        def slot(self, ref, step, by):
            at = self.base + slot_rows(self.plan[:step]) + (by - 1) * self.plan[step][2]
            return ref.at[self.layer, pl.ds(at, self.plan[step][2])]

        def at(self, off, size):
            return pl.ds(pl.multiple_of(off, ALIGN), size)

        def start(self, step):
            bit, size, share, split = self.plan[step]
            mine = place(bit, size)
            self.copies = []
            for by in range(1, size):
                away = self.off + (mine + by) % size * share if split else self.off
                src = self.slot(red_send, step, by)
                src[...] = grads[self.layer, self.at(away, share), :].astype(BF16)
                self.copies.append(remote(src, self.slot(red_recv, step, by), peer(bit, size, by)))
            if self.gains is not None:
                self.gains.start(step)

        def finish(self, step):
            bit, size, share, split = self.plan[step]
            if split:
                self.off = self.off + place(bit, size) * share
                self.left.append((bit, size, self.off, share))
                summed = grads[self.layer, self.at(self.off, share), :]
            else:
                summed = self.slot(red_send, step, 1)[...].astype(F32)
            for copy in self.copies:
                copy.wait()
            for by in range(1, size):
                summed = summed + self.slot(red_recv, step, by)[...].astype(F32)
            if step + 1 < len(self.plan):
                grads[self.layer, self.at(self.off, share), :] = summed
            else:
                full[self.layer, self.at(self.off, share), :] = summed.astype(BF16)
            if self.gains is not None:
                self.gains.finish(step)

        def flow(self):
            for step in range(len(self.plan)):
                self.start(step)
                yield
                self.finish(step)
            for bit, size, off, share in reversed(self.left):
                region = full.at[self.layer, self.at(off, share)]
                copies = [remote(region, region, peer(bit, size, by)) for by in range(1, size)]
                yield
                for copy in copies:
                    copy.wait()
            done = full.at[self.layer, pl.ds(self.which * width, width)]
            targets = (out_grad_hbm, self_grad_hbm, agg_grad_hbm)
            last.append(local(done, targets[self.which].at[self.layer]))

    class Gains:
        def __init__(self, value):
            self.value, self.used = value, 0

        def start(self, step):
            bit, size = orders[0][step]
            self.copies = []
            self.slots = range(self.used, self.used + size - 1)
            self.used += size - 1
            gain_send[step] = self.value
            for by, slot in enumerate(self.slots, 1):
                self.copies.append(
                    remote(gain_send.at[step], gain_recv.at[slot], peer(bit, size, by))
                )

        def finish(self, step):
            bit, size = orders[0][step]
            for copy in self.copies:
                copy.wait()
            if size == 2:
                self.value = self.value + gain_recv[self.slots[0]]
                return
            mine = place(bit, size)
            terms = [self.value] + [gain_recv[slot] for slot in self.slots]
            total = jnp.zeros_like(self.value)
            for want in range(size):
                for by in range(size):
                    total = total + jnp.where((mine - by + size) % size == want, 1.0, 0.0) * terms[by]
            self.value = total

    flows = []

    def advance():
        for item in list(flows):
            try:
                next(item)
            except StopIteration:
                flows.remove(item)

    gains = None
    last = []

    def begin(layer, which, left, right):
        grads[layer, pl.ds(which * width, width), :] = dot(left, right, 0, 0)
        last = gains if layer == 0 and which == 2 else None
        flows.append(Reducer(layer, which, last).flow())
        next(flows[-1])

    get_cotan.wait()
    grad = cotan[...].astype(F32)
    gain_rows = lax.broadcasted_iota(jnp.int32, gain_send.shape[1:], 0)
    gain_total = jnp.zeros(gain_send.shape[1:], F32)
    grad_copy = None
    for layer in reversed(range(layers)):
        n = normed[layer]
        masked = grad * mask
        scaled = masked * gain_vm[pl.ds(layer, 1), :]
        lifted = inv_std[layer] * (
            scaled
            - jnp.mean(scaled, axis=-1, keepdims=True)
            - n * jnp.mean(scaled * n, axis=-1, keepdims=True)
        )
        lifted = lifted.astype(BF16)
        if layer == 0:
            begin(layer, 0, hidden[layer], lifted)
        back = dot(lifted, wout[layer], 1, 1)
        pre_grad = (back * sig_grad[layer]).astype(BF16)
        gain_term = jnp.sum(masked * n, axis=0, keepdims=True)
        gain_total = jnp.where(gain_rows == layer, gain_term, gain_total)
        if layer == 0:
            gains = Gains(gain_total)
            begin(layer, 1, ext[layer, pl.ds(0, rows), :], pre_grad)
            begin(layer, 2, agg[layer], pre_grad)
        agg_back = dot(pre_grad, wagg[layer], 1, 1).astype(BF16)
        spread = dot(adj[:, pl.ds(rows, rows + 2 * blk)], agg_back, 0, 0)
        back_send[layer] = spread.astype(BF16)
        first = AcrossCopy(
            back_send.at[layer, pl.ds(0, blk)], back_recv.at[layer, pl.ds(0, blk)]
        )
        rest = pl.ds(blk, rows + blk)
        second = remote(back_send.at[layer, rest], back_recv.at[layer, rest], sibling)
        if layer > 0:
            begin(layer, 0, hidden[layer], lifted)
            begin(layer, 1, ext[layer, pl.ds(0, rows), :], pre_grad)
            begin(layer, 2, agg[layer], pre_grad)
        grad = masked + dot(pre_grad, wself[layer], 1, 1)
        grad += dot(adj[:, pl.ds(0, rows)], agg_back, 0, 0)
        advance()
        first.wait()
        second.wait()
        from_other = back_recv[layer, pl.ds(0, blk), :].astype(F32)
        from_sibling = back_recv[layer, pl.ds(blk, blk), :].astype(F32)
        pieces = [
            hot(to_other, j) * from_other + hot(to_sibling, j) * from_sibling
            for j in range(nblocks)
        ]
        grad += back_recv[layer, pl.ds(2 * blk, rows), :].astype(F32)
        grad += jnp.concatenate(pieces, axis=0)
    feats_grad[...] = (grad * mask).astype(BF16)
    grad_copy = local(feats_grad, feats_grad_hbm)
    while flows:
        advance()
    gain_grad_vm[...] = gains.value[0:layers]

    for copy in last:
        copy.wait()
    out_copy.wait()
    grad_copy.wait()
    assert sems.used <= sem_count, sems.used


def copy_kernel(*refs):
    count = len(refs) // 3
    sources, targets, stages, sem = refs[:count], refs[count : 2 * count], refs[2 * count : -1], refs[-1]
    chunks = []
    for refs_here in zip(sources, stages, targets):
        if len(refs_here[0].shape) == 3:
            chunks += [tuple(ref.at[i] for ref in refs_here) for i in range(refs_here[0].shape[0])]
        else:
            chunks.append(refs_here)
    loads, stores = [], []
    for i, (source, stage, _) in enumerate(chunks):
        loads.append(pltpu.make_async_copy(source, stage, sem.at[0, i]))
        loads[-1].start()
    for i, (_, stage, target) in enumerate(chunks):
        loads[i].wait()
        stores.append(pltpu.make_async_copy(stage, target, sem.at[1, i]))
        stores[-1].start()
    for store in stores:
        store.wait()


def copied_out(arrays):
    return pl.pallas_call(
        copy_kernel,
        out_shape=tuple(jax.ShapeDtypeStruct(x.shape, x.dtype) for x in arrays),
        in_specs=[pl.BlockSpec(memory_space=pl.ANY)] * len(arrays),
        out_specs=(pl.BlockSpec(memory_space=pl.ANY),) * len(arrays),
        scratch_shapes=[pltpu.VMEM(x.shape, x.dtype) for x in arrays]
        + [pltpu.SemaphoreType.DMA((2, sum(x.shape[0] if x.ndim == 3 else 1 for x in arrays)))],
    )(*arrays)


def per_device(
    count,
    node_feats,
    cotangent,
    tile_val,
    tile_src,
    halo_list,
    block_count,
    coarse_src,
    coarse_val,
    w_self,
    w_agg,
    w_out,
    norm_gain,
):
    rows, width = node_feats.shape
    nblocks, ktiles, blk, _ = tile_val.shape
    layers = w_self.shape[0]
    orders = group_orders(count)
    stages = len(orders[0])
    links = sum(size - 1 for _, size in orders[0])
    plans = [reduce_plan(rows, order) for rows, order in zip(part_rows(width), orders)]
    reduce_rows = sum(slot_rows(plan) for plan in plans)
    sem_count = 32 + 14 * layers + 4 * len(plans) * layers * links + 2 * links
    ext_rows = 2 * rows + 2 * blk
    any_space = pl.BlockSpec(memory_space=pl.ANY)
    smem = pl.BlockSpec(memory_space=pltpu.SMEM)
    vmem = pl.BlockSpec(memory_space=pltpu.VMEM)
    shape = jax.ShapeDtypeStruct
    weights = (layers, width, width)
    outs = pl.pallas_call(
        functools.partial(kernel, count, sem_count),
        out_shape=(
            shape((rows, width), BF16),
            shape((rows, width), BF16),
            shape(weights, BF16),
            shape(weights, BF16),
            shape(weights, BF16),
            shape((layers, width), F32),
        ),
        in_specs=[smem] * 5 + [any_space] * 6 + [vmem],
        out_specs=(any_space,) * 5 + (vmem,),
        scratch_shapes=[
            pltpu.VMEM((rows, width), BF16),
            pltpu.VMEM((rows, width), BF16),
            pltpu.VMEM(tile_val.shape, BF16),
            pltpu.VMEM(weights, BF16),
            pltpu.VMEM(weights, BF16),
            pltpu.VMEM(weights, BF16),
            pltpu.VMEM((rows, ext_rows), BF16),
            pltpu.VMEM((layers, ext_rows, width), BF16),
            pltpu.VMEM((layers, 2 * blk, width), BF16),
            pltpu.VMEM((layers, rows, width), BF16),
            pltpu.VMEM((layers, rows, width), F32),
            pltpu.VMEM((layers, rows, width), BF16),
            pltpu.VMEM((layers, rows, width), F32),
            pltpu.VMEM((layers, rows, 1), F32),
            pltpu.VMEM((rows, width), BF16),
            pltpu.VMEM((rows, width), BF16),
            pltpu.VMEM((layers, rows + 2 * blk, width), BF16),
            pltpu.VMEM((layers, rows + 2 * blk, width), BF16),
            pltpu.VMEM((layers, 3 * width, width), F32),
            pltpu.VMEM((layers, reduce_rows, width), BF16),
            pltpu.VMEM((layers, reduce_rows, width), BF16),
            pltpu.VMEM((layers, 3 * width, width), BF16),
            pltpu.VMEM((stages, 8, width), F32),
            pltpu.VMEM((links, 8, width), F32),
            pltpu.SemaphoreType.DMA((sem_count,)),
        ],
        compiler_params=pltpu.CompilerParams(
            collective_id=0, has_side_effects=True, vmem_limit_bytes=63 * 2**20
        ),
        cost_estimate=pl.CostEstimate(
            flops=3 * 10**9, bytes_accessed=10 * 2**20, transcendentals=2 * layers * rows * width
        ),
    )(
        tile_src,
        halo_list,
        block_count,
        coarse_src,
        coarse_val,
        node_feats,
        cotangent,
        tile_val,
        w_self,
        w_agg,
        w_out,
        norm_gain,
    )
    return copied_out(outs)


def solution(mesh):
    nodes = P(("groups", "gx"), None)
    return jax.shard_map(
        functools.partial(per_device, mesh.shape["gx"]),
        mesh=mesh,
        in_specs=(
            nodes,
            nodes,
            P(("groups", "gx"), None, None, None),
            nodes,
            P(("groups", "gx"), None, None),
            P(("groups", "gx")),
            nodes,
            nodes,
            P(),
            P(),
            P(),
            P(),
        ),
        out_specs=(
            nodes,
            nodes,
            P("groups", None, None),
            P("groups", None, None),
            P("groups", None, None),
            P("groups", None),
        ),
        check_vma=False,
    )
```
